32 devices in a mesh: dp: 4 (over z), width: 4 (over y, x), heads: 2 (over core).
Axes of the slice: x: 2, y: 2, z: 4, core: 2. Of those that a mesh axis runs over, the one named last changes fastest.
Arguments:
- inputs: bfloat16 [8192, 768], P(('dp', 'width')), may hold values from -6 to 6
- seq_lengths: int32 [4, 3], P('dp'), may hold values from 1 to 1537, 2048 in all within a row
- routes: int32 [8192, 2], P(('dp', 'width')), may hold values from 0 to 7, all different within a row; in each aligned block of 512 rows (0 to 511, 512 to 1023, ...) at most 256 rows name the same one
- norm_one: bfloat16 [768], P('width'), may hold values from 0.5 to 1.5
- qkv_weight: bfloat16 [3, 768, 768], P(None, 'width', 'heads'), may hold values from -0.21875 to 0.21875
- slopes: float32 [12], P('heads'), may hold values from 0.05 to 1
- out_weight: bfloat16 [768, 768], P('heads', 'width'), may hold values from -0.75 to 0.75
- norm_two: bfloat16 [768], P('width'), may hold values from 0.5 to 1.5
- router: bfloat16 [768, 8], P('width'), may hold values from -0.15625 to 0.15625
- expert_in: bfloat16 [8, 768, 3072], P('dp', 'width', 'heads'), may hold values from -0.21875 to 0.21875
- expert_out: bfloat16 [8, 3072, 768], P('dp', 'heads', 'width'), may hold values from -0.109375 to 0.109375
- cotangent: bfloat16 [8192, 768], P(('dp', 'width')), may hold values from -6 to 6
Outputs:
- mixed_out: bfloat16 [8192, 768], P(('dp', 'width'))
- input_grad: float32 [8192, 768], P(('dp', 'width'))
- norm_one_grad: float32 [768], P('width')
- qkv_grad: float32 [3, 768, 768], P(None, 'width', 'heads')
- slope_grad: float32 [12], P('heads')
- out_grad: float32 [768, 768], P('heads', 'width')
- norm_two_grad: float32 [768], P('width')
- router_grad: float32 [768, 8], P('width')
- expert_in_grad: float32 [8, 768, 3072], P('dp', 'width', 'heads')
- expert_out_grad: float32 [8, 3072, 768], P('dp', 'heads', 'width')
The draws below stay inside these ranges and needn't reach their ends.
Inputs may be any that keep to these rules, and one draw needn't show every extreme that they name: `routes`: each row names two different experts. In each aligned block of 512 rows (the rows of one device), no expert is named more than 256 times, and in every draw some block names some expert exactly 256 times. `seq_lengths`: each row of 3 lengths sums to 2048, and its largest is exactly 1537.
All inputs are finite; a program needn't handle non-finite values.
Results may differ from the reference program's by a relative error of at most 0.013.
Values may be sent and summed in bfloat16 or wider, within the bound.
A program may use at most 192 MiB of HBM per device.

```python
import math
import jax
import jax.numpy as jnp
import numpy as np
from jax import lax

D = 768
H = 12
HD = 64
FF = 3072
TOK_DEV = 2048
SEQS = 3
TOKENS = 8192
TW = 512
E = 8
CAP = 256
LONGEST = 1537
N_DP = 4
N_WIDTH = 4
N_HEADS = 2


def level_of(stream_key, dims, pieces, low, top_value):
    level = 1.0
    for dim, blocks in pieces:
        heights = jax.random.uniform(jax.random.fold_in(jax.random.fold_in(stream_key, 6), dim), (blocks,), jnp.float32, low / len(pieces), top_value / len(pieces))
        level = level * jnp.repeat(jnp.exp(heights), dims[dim] // blocks).reshape((-1,) + (1,) * (len(dims) - 1 - dim))
    return level


def profile(number_of, total, bound, skew):
    loads = [(1 << 20) // math.isqrt(rank ** skew) + 1 for rank in range(2, number_of + 1)]
    surplus, given = total - bound - (number_of - 1), [1] * (number_of - 1)
    while surplus > 0:
        free = [i for i in range(number_of - 1) if given[i] < bound]
        whole, remaining = sum([loads[i] for i in free]), surplus
        for i in free:
            more = min(bound - given[i], max(1, remaining * loads[i] // whole), surplus)
            given[i] = given[i] + more
            surplus = surplus - more
    return np.array([bound] + given)


def uneven(own_key, amount, total, reach, slope):
    if amount == 2:
        one = jax.random.randint(own_key, (), max(1, total - reach), min(reach, total - 1) + 1)
        return jnp.stack([one, total - one])
    lengths = jnp.asarray(profile(amount, total, reach, slope), jnp.int32)
    pairs = (amount - 1) // 2
    donor, sink = lengths[1:1 + 2 * pairs:2], lengths[2:2 + 2 * pairs:2]
    slack = jnp.minimum(donor - 1, reach - sink)
    passed = jax.random.randint(jax.random.fold_in(own_key, 1), (pairs,), 0, 1 << 20) % (slack + 1)
    lengths = lengths.at[1:1 + 2 * pairs:2].set(donor - passed).at[2:2 + 2 * pairs:2].set(sink + passed)
    return lengths[jax.random.permutation(jax.random.fold_in(own_key, 2), amount)]


def shared_out(own_key, own, number, rows, count, top, bound, slope):
    ranking = jax.random.permutation(own_key, count)
    crowded, usual = shares(count, rows * top, bound, slope, True), shares(count, rows * top, bound, slope, False)
    places = jnp.arange(count)

    def named(lengths, offset_by):
        used = int((lengths > 0).sum())
        fixed = max(1, used // 4)
        passed = fixed + (places - fixed + offset_by * (used - fixed)) % max(1, count - fixed)
        return jnp.zeros((count,), jnp.int32).at[ranking[jnp.where(places < fixed, places, passed)]].set(jnp.asarray(lengths, jnp.int32))

    lengths = jnp.where(number % 4 == 0, named(crowded, number // 4), named(usual, number - number // 4 - 1))
    mixed = jax.random.permutation(jax.random.fold_in(own, 3), count)
    giver, taker = mixed[0:count // 2 * 2:2], mixed[1:count // 2 * 2:2]
    margin = jnp.minimum(lengths[giver] - 1, bound - lengths[taker]) // 2
    margin = jnp.where((giver == ranking[0]) | (taker == ranking[0]) | (lengths[taker] == 0), 0, jnp.maximum(margin, 0))
    passed = jax.random.randint(jax.random.fold_in(own, 4), (count // 2,), 0, 1 << 20) % (margin + 1)
    lengths = lengths.at[giver].add(-passed).at[taker].add(passed)
    items = jnp.searchsorted(jnp.cumsum(lengths), jnp.arange(rows * top), side="right").astype(jnp.int32)
    grid = items.reshape(top, rows).T
    grid = grid[jax.random.permutation(jax.random.fold_in(own, 1), rows)]
    offset_by = jax.random.randint(jax.random.fold_in(own, 2), (rows, 1), 0, top)
    return jnp.take_along_axis(grid, (jnp.arange(top)[None, :] + offset_by) % top, axis=1)


def shares(number_of, total, limit, lean, full):
    loads = [(1 << 20) // math.isqrt(rank ** lean) + 1 for rank in range(1, number_of + 1)]
    largest = limit if full else min(limit, max(-(-total // number_of), total * loads[0] // sum(loads)))
    least = 1 if total - largest >= number_of - 1 else 0
    given, spare = [largest] + [least] * (number_of - 1), total - largest - least * (number_of - 1)
    while spare > 0:
        free = [i for i in range(1, number_of) if given[i] < largest] or [i for i in range(1, number_of) if given[i] < limit]
        pool, remaining = sum([loads[i] for i in free]), spare
        for i in free:
            extra = min(limit - given[i], max(1, remaining * loads[i] // pool), spare)
            given[i] = given[i] + extra
            spare = spare - extra
    return np.array(given)


def gaussian(rng, shape, width, most, split=(), kind=jnp.bfloat16):
    gain = level_of(rng, shape, split, -0.22, 0.18) if split else 1.0
    drawn = jax.random.normal(rng, shape, jnp.float32) * width * gain
    return jnp.minimum(jnp.maximum(drawn, -most), most).astype(kind)


def setup_inputs(seed: int = 0) -> dict:
    keys = jax.random.split(jax.random.key(seed), 13)
    inputs = gaussian(keys[0], (TOKENS, D), 1.0, 6.0, ((0, 16),))
    seq_lengths = jax.vmap(lambda own: uneven(own, SEQS, TOK_DEV, LONGEST, 2))(jax.random.split(keys[1], N_DP)).reshape((N_DP, SEQS)).astype(jnp.int32)
    routes_keys = jax.random.split(jax.random.fold_in(keys[2], 1), TOKENS // TW)
    routes_turns = jax.random.permutation(jax.random.fold_in(keys[2], 3), TOKENS // TW)
    routes = jax.vmap(lambda own, number: shared_out(jax.random.fold_in(keys[2], 2), own, number, TW, E, 2, CAP, 2))(routes_keys, routes_turns).reshape((TOKENS, 2))
    norm_one = jnp.clip(1.0 + 0.1 * jax.random.normal(keys[3], (D,), jnp.float32), 0.5, 1.5).astype(jnp.bfloat16)
    qkv_weight = gaussian(keys[4], (3, D, H * HD), D ** -0.5, 0.21875, ((1, 4), (2, 2)))
    slopes = jnp.clip(jnp.exp(math.log(1.0) - 2.9957323 * jax.random.uniform(keys[5], (H,), jnp.float32) ** level_of(keys[5], (H,), ((0, 2),), -0.2, 0.2)), 0.05, 1.0)
    out_weight = gaussian(keys[6], (H * HD, D), HD ** -0.5, 0.75, ((0, 2), (1, 4)))
    norm_two = jnp.clip(1.0 + 0.1 * jax.random.normal(keys[7], (D,), jnp.float32), 0.5, 1.5).astype(jnp.bfloat16)
    router = gaussian(keys[8], (D, E), (D * 16 // 9) ** -0.5, 0.15625, ((0, 4),))
    expert_in = gaussian(keys[9], (E, D, FF), D ** -0.5, 0.21875, ((0, 4), (1, 4), (2, 2)))
    expert_out = gaussian(keys[10], (E, FF, D), FF ** -0.5, 0.109375, ((0, 4), (1, 2), (2, 4)))
    cotangent = gaussian(keys[11], (TOKENS, D), 1.0, 6.0, ((0, 16),))
    return {"inputs": inputs, "seq_lengths": seq_lengths, "routes": routes, "norm_one": norm_one, "qkv_weight": qkv_weight, "slopes": slopes, "out_weight": out_weight, "norm_two": norm_two, "router": router, "expert_in": expert_in, "expert_out": expert_out, "cotangent": cotangent}


@jax.custom_vjp
def low(v):
    return lax.optimization_barrier(v.astype(jnp.bfloat16)).astype(jnp.float32)

@jax.custom_vjp
def low_back(v):
    return v

def low_keep(v):
    return (low(v), None)

def low_pass(kept, grad):
    return (grad,)

def back_keep(v):
    return (v, None)

def back_low(kept, grad):
    return (low(grad),)
low.defvjp(low_keep, low_pass)
low_back.defvjp(back_keep, back_low)
epsilon = 1e-06
highest = lax.Precision.HIGHEST

def rms_norm(values, gain_vec):
    return values * lax.rsqrt(lax.optimization_barrier(jnp.mean(values * values, axis=-1, keepdims=True)) + epsilon) * gain_vec

def segment_ids(length_row):
    seq_ends = jnp.cumsum(length_row).astype(jnp.int32)
    positions = jnp.arange(TOK_DEV, dtype=jnp.int32)
    return lax.optimization_barrier(jnp.sum((positions[:, None] >= seq_ends[None, :]).astype(jnp.int32), axis=1)).astype(jnp.int32)

def attention(queries, keys_all, values_all, seq_lengths, slope_vals):
    block_rows = min(512, TOK_DEV)
    scale_factor = 1.0 / math.sqrt(HD)
    key_pos = jnp.arange(TOK_DEV, dtype=jnp.int32)

    def one_block(block_num):
        row_start = (block_num * block_rows).astype(jnp.int32)
        pack_num = (row_start // TOK_DEV).astype(jnp.int32)
        pack_start = (pack_num * TOK_DEV).astype(jnp.int32)
        query_blk = lax.dynamic_slice_in_dim(queries, row_start, block_rows, 0).reshape(block_rows, H, HD)
        keys_pack = lax.dynamic_slice_in_dim(keys_all, pack_start, TOK_DEV, 0).reshape(TOK_DEV, H, HD)
        values_pack = lax.dynamic_slice_in_dim(values_all, pack_start, TOK_DEV, 0).reshape(TOK_DEV, H, HD)
        seg_all = segment_ids(seq_lengths[pack_num])
        offset_in = (row_start - pack_start).astype(jnp.int32)
        query_pos = offset_in + jnp.arange(block_rows, dtype=jnp.int32)
        seg_query = lax.dynamic_slice_in_dim(seg_all, offset_in, block_rows, 0)
        distance = jnp.maximum(query_pos[:, None] - key_pos[None, :], 0)
        decay_term = jnp.log1p(distance.astype(jnp.float32))
        allowed = (seg_query[:, None] == seg_all[None, :]) & (key_pos[None, :] <= query_pos[:, None])
        raw_scores = jnp.einsum('qhd,khd->hqk', query_blk, keys_pack, precision=highest) * scale_factor
        scores = low_back(raw_scores - slope_vals[:, None, None] * decay_term[None])
        scores = jnp.where(allowed[None], scores, -1e+30)
        top_score = lax.optimization_barrier(jnp.max(scores, axis=-1, keepdims=True))
        weights = jnp.exp(scores - top_score)
        weights = weights / lax.optimization_barrier(jnp.sum(weights, axis=-1, keepdims=True))
        mixed_blk = jnp.einsum('hqk,khd->qhd', low(weights), values_pack, precision=highest)
        return mixed_blk.reshape(block_rows, H * HD)
    block_ids = jnp.arange(TOKENS // block_rows, dtype=jnp.int32)
    return lax.map(jax.checkpoint(one_block), block_ids).reshape(TOKENS, H * HD)

def slot_table(routes):
    blocks = N_DP * N_WIDTH
    flat_ids = routes.reshape(blocks, 2 * TW)
    onehot = (flat_ids[:, :, None] == jnp.arange(E, dtype=jnp.int32)[None, None, :]).astype(jnp.int32)
    slot_rank = lax.optimization_barrier(jnp.sum((jnp.cumsum(onehot, axis=1).astype(jnp.int32) - onehot) * onehot, axis=2)).astype(jnp.int32)
    block_ids = jnp.arange(blocks, dtype=jnp.int32)[:, None]
    target = flat_ids * (blocks * CAP) + block_ids * CAP + slot_rank
    pair_ids = jnp.arange(blocks * 2 * TW, dtype=jnp.int32)
    slot_owner = jnp.zeros((E * blocks * CAP,), jnp.int32).at[target.reshape(-1)].set(pair_ids + 1)
    return slot_owner.reshape(E, blocks * CAP)

def expert_mix(xn_two, gate_vals, w_first, w_second, slot_owner):
    flat_gates = gate_vals.reshape(-1)
    half_width = FF // N_HEADS

    def one_expert(running, operands):
        first_one, second_one, entries = operands
        is_live = (entries > 0).astype(jnp.float32)
        pair_idx = jnp.maximum(entries - 1, 0)
        token_idx = pair_idx // 2
        row_vals = xn_two[token_idx] * is_live[:, None]
        summed = jnp.zeros((row_vals.shape[0], D), jnp.float32)
        for half_num in range(N_HEADS):
            inputs = low_back(row_vals)
            pre_act = low_back(jnp.dot(inputs, first_one[:, half_num * half_width:(half_num + 1) * half_width], precision=highest))
            activated = low(jax.nn.gelu(pre_act))
            summed = summed + low_back(low(jnp.dot(activated, second_one[half_num * half_width:(half_num + 1) * half_width], precision=highest)))
        weight_col = flat_gates[pair_idx] * is_live
        return (running.at[token_idx].add(weight_col[:, None] * summed), None)
    result, unused = lax.scan(jax.checkpoint(one_expert), jnp.zeros((TOKENS, D), jnp.float32), (w_first, w_second, slot_owner))
    return result

def reference(inputs, seq_lengths, routes, norm_one, qkv_weight, slopes, out_weight, norm_two, router, expert_in, expert_out, cotangent):
    slot_owner = slot_table(routes)

    def forward(x_in, gain_one, w_qkv, slope_vals, w_proj, gain_two, w_route, w_first, w_second):
        xn_one = low(rms_norm(x_in, gain_one))
        qkv_vals = jnp.einsum('td,jdc->jtc', xn_one, w_qkv, precision=highest)
        queries = low_back(low(qkv_vals[0]))
        keys_all = low_back(low(qkv_vals[1]))
        values_all = low_back(low(qkv_vals[2]))
        attended = low_back(low(attention(queries, keys_all, values_all, seq_lengths, slope_vals)))
        hidden_one = x_in + low_back(jnp.dot(attended, w_proj, precision=highest))
        xn_two = low(rms_norm(hidden_one, gain_two))
        logits = jnp.dot(xn_two, w_route, precision=highest)
        chosen = jnp.take_along_axis(logits, routes, axis=1)
        gate_exp = jnp.exp(chosen - lax.optimization_barrier(jnp.max(chosen, axis=1, keepdims=True)))
        gate_vals = gate_exp / lax.optimization_barrier(jnp.sum(gate_exp, axis=1, keepdims=True))
        return hidden_one + expert_mix(xn_two, gate_vals, w_first, w_second, slot_owner)
    floats = (inputs.astype(jnp.float32), norm_one.astype(jnp.float32), qkv_weight.astype(jnp.float32), slopes.astype(jnp.float32), out_weight.astype(jnp.float32), norm_two.astype(jnp.float32), router.astype(jnp.float32), expert_in.astype(jnp.float32), expert_out.astype(jnp.float32))
    output, pullback = jax.vjp(forward, *floats)
    gradients = pullback(cotangent.astype(jnp.float32))
    return (output.astype(jnp.bfloat16), gradients[0], gradients[1], gradients[2], gradients[3], gradients[4], gradients[5], gradients[6], gradients[7], gradients[8])
```

```python
import math

import jax
import jax.numpy as jnp
from jax import lax
from jax.sharding import PartitionSpec as P

D = 768
HD = 64


epsilon = 1e-06
highest = lax.Precision.HIGHEST


def rms_norm(values, gain_vec):
    return (
        values * lax.rsqrt(jnp.mean(values * values, axis=-1, keepdims=True) + epsilon) * gain_vec
    )


def pair_of(array, num):
    return array[:, 2 * HD * num : 2 * HD * (num + 1)].reshape(array.shape[0], 2, HD)


def pair_scores(query_blk, keys_pair, slope_pair, decay_term):
    raw_scores = jnp.einsum("qhd,khd->hqk", query_blk, keys_pair, preferred_element_type=jnp.float32)
    return raw_scores * (1.0 / math.sqrt(HD)) - slope_pair[:, None, None] * decay_term[None]


def pair_probs(scores):
    exp_scores = jnp.exp(scores - jnp.max(scores, axis=-1, keepdims=True))
    return exp_scores / jnp.sum(exp_scores, axis=-1, keepdims=True)


def attend(queries, keys_all, values_all, slopes, decay_term):
    out_cols = []
    for num in range(queries.shape[1] // (2 * HD)):
        scores = pair_scores(
            pair_of(queries, num), pair_of(keys_all, num), slopes[2 * num : 2 * num + 2], decay_term
        )
        out_cols.append(
            jnp.einsum(
                "hqk,khd->qhd",
                pair_probs(scores).astype(jnp.bfloat16),
                pair_of(values_all, num),
                preferred_element_type=jnp.float32,
            ).reshape(queries.shape[0], 2 * HD)
        )
    return jnp.concatenate(out_cols, axis=1).astype(jnp.bfloat16)


def attend_back(queries, keys_all, values_all, slopes, decay_term, grad_att):
    scale = 1.0 / math.sqrt(HD)
    grad_cols = ([], [], [])
    slope_cols = []

    def flat(values):
        return values.reshape(values.shape[0], 2 * HD).astype(jnp.bfloat16)

    for num in range(queries.shape[1] // (2 * HD)):
        query_blk, keys_pair, values_pair, grad_blk = [
            pair_of(array, num) for array in (queries, keys_all, values_all, grad_att)
        ]
        probs = pair_probs(
            pair_scores(query_blk, keys_pair, slopes[2 * num : 2 * num + 2], decay_term)
        )
        grad_probs = jnp.einsum(
            "qhd,khd->hqk", grad_blk, values_pair, preferred_element_type=jnp.float32
        )
        row_sum = jnp.sum(probs * grad_probs, axis=-1, keepdims=True)
        grad_scores = (probs * (grad_probs - row_sum)).astype(jnp.bfloat16)
        query_part = jnp.einsum(
            "hqk,khd->qhd", grad_scores, keys_pair, preferred_element_type=jnp.float32
        )
        key_part = jnp.einsum(
            "hqk,qhd->khd", grad_scores, query_blk, preferred_element_type=jnp.float32
        )
        value_part = jnp.einsum(
            "hqk,qhd->khd",
            probs.astype(jnp.bfloat16),
            grad_blk,
            preferred_element_type=jnp.float32,
        )
        grad_cols[0].append(flat(query_part * scale))
        grad_cols[1].append(flat(key_part * scale))
        grad_cols[2].append(flat(value_part))
        slope_cols.append(
            -jnp.sum(grad_scores.astype(jnp.float32) * decay_term[None], axis=(1, 2))
        )
    return (
        *[jnp.concatenate(cols, axis=1) for cols in grad_cols],
        jnp.concatenate(slope_cols),
    )


def swap_pairs(axis, step):
    return [(i, i ^ step) for i in range(lax.axis_size(axis))]


def hop(values, axis, step):
    return lax.ppermute(values, axis, swap_pairs(axis, step))


def pieces_of(values, axis):
    return [values] + [hop(values, axis, s) for s in range(1, lax.axis_size(axis))]


def summed_pieces(chunks, axis):
    total = chunks[0].astype(jnp.float32)
    for s in range(1, lax.axis_size(axis)):
        total = total + hop(chunks[s], axis, s).astype(jnp.float32)
    return total


def summed_everywhere(values, axis):
    step = 1
    while step < lax.axis_size(axis):
        values = values + hop(values, axis, step)
        step *= 2
    return values


def xor_columns(values, count, index):
    width = values.shape[-1] // count
    bit = 1
    while bit < count:
        blocks = [values[..., (i ^ bit) * width : ((i ^ bit) + 1) * width] for i in range(count)]
        values = jnp.where((index & bit) > 0, jnp.concatenate(blocks, axis=-1), values)
        bit *= 2
    return values


def own_half_first(values, head_index, axis):
    half = values.shape[axis] // 2
    low_half = lax.slice_in_dim(values, 0, half, axis=axis)
    high_half = lax.slice_in_dim(values, half, 2 * half, axis=axis)
    return jnp.where(head_index == 0, values, jnp.concatenate([high_half, low_half], axis=axis))


def rows_everywhere(values, half):
    found = [values]
    for s in range(1, lax.axis_size("dp")):
        piece = hop(values[:half], "dp", s)
        found.append(jnp.concatenate([piece, hop(piece, "heads", 1)], axis=0))
    return jnp.stack(found)


def rows_returned(picks, slot_rows, half):
    mine, theirs = [
        jnp.einsum("sct,scd->std", part, slot_rows, preferred_element_type=jnp.float32)
        for part in (picks[:, :, :half], picks[:, :, half:])
    ]
    theirs = hop(theirs.astype(jnp.bfloat16), "heads", 1)
    chunks = (mine + theirs.astype(jnp.float32)).astype(jnp.bfloat16)
    return summed_pieces([chunks[s] for s in range(chunks.shape[0])], "dp")


def both_halves(own, head_index):
    other = hop(own, "heads", 1)
    return jnp.where(
        head_index == 0,
        jnp.concatenate([own, other], axis=0),
        jnp.concatenate([other, own], axis=0),
    )


def beside(values):
    half = values.shape[0] // 2
    return jnp.concatenate([values[:half], values[half:]], axis=1)


def unbeside(values):
    half = values.shape[1] // 2
    return jnp.concatenate([values[:, :half], values[:, half:]], axis=0)


def shards(
    inputs,
    seq_lengths,
    routes,
    norm_one,
    qkv_weight,
    slopes,
    out_weight,
    norm_two,
    router,
    expert_in,
    expert_out,
    cotangent,
):
    rows_own = inputs.shape[0]
    half = rows_own // 2
    width_count = lax.axis_size("width")
    dp_count = lax.axis_size("dp")
    width_index = lax.axis_index("width")
    dp_index = lax.axis_index("dp")
    head_index = lax.axis_index("heads")
    expert_total = router.shape[1]
    local_experts = expert_in.shape[0]
    slot_cap = 4 * rows_own // expert_total
    block_d = norm_one.shape[0]
    heads_cols = qkv_weight.shape[2]

    small = jnp.concatenate([router.T, norm_one[None], norm_two[None]], axis=0)
    small = beside(small)
    small_rows = small.shape[0]
    pack = jnp.concatenate(
        [
            qkv_weight.reshape(3 * block_d, heads_cols),
            beside(out_weight),
            jnp.pad(small, ((0, -small_rows % 16), (0, 0))),
        ],
        axis=0,
    )
    packs = pieces_of(pack, "width")
    out_from = 3 * block_d
    small_from = out_from + out_weight.shape[0] // 2
    w_qkv = jnp.concatenate(
        [piece[:out_from].reshape(3, block_d, heads_cols) for piece in packs], axis=1
    )
    w_proj = jnp.concatenate([unbeside(piece[out_from:small_from]) for piece in packs], axis=1)
    smalls = jnp.concatenate(
        [unbeside(piece[small_from : small_from + small_rows]) for piece in packs], axis=1
    )
    w_route_t = smalls[:expert_total]
    gain_one = smalls[expert_total].astype(jnp.float32)
    gain_two = smalls[expert_total + 1].astype(jnp.float32)

    x_vals = xor_columns(inputs, width_count, width_index).astype(jnp.float32)
    cot = xor_columns(cotangent, width_count, width_index)
    grad_out = cot.astype(jnp.float32)
    norm_first, back_first = jax.vjp(rms_norm, x_vals, gain_one)
    xn_one = norm_first.astype(jnp.bfloat16)
    qkv_vals = jnp.einsum("rd,jdc->jrc", xn_one, w_qkv, preferred_element_type=jnp.float32).astype(
        jnp.bfloat16
    )
    queries = qkv_vals[0]
    kv_pieces = pieces_of(qkv_vals[1:], "width")
    expert_stack = jnp.concatenate(
        [expert_in, jnp.swapaxes(expert_out, 1, 2).astype(jnp.bfloat16)], axis=0
    )
    kv_pieces, expert_stack = lax.optimization_barrier((kv_pieces, expert_stack))
    key_value = jnp.concatenate(kv_pieces, axis=1)
    keys_all = key_value[0]
    values_all = key_value[1]
    stacks = pieces_of(expert_stack, "width")
    w_first = [
        jnp.concatenate([piece[e] for piece in stacks], axis=0) for e in range(local_experts)
    ]
    w_second_t = [
        jnp.concatenate([piece[local_experts + e] for piece in stacks], axis=0)
        for e in range(local_experts)
    ]

    cot_rows_all = rows_everywhere(own_half_first(cot, head_index, 0), half)
    routes_own = own_half_first(routes.T, head_index, 1)
    routes_all = jnp.stack(pieces_of(routes_own, "dp"))

    row_ids = jnp.arange(rows_own, dtype=jnp.int32)
    query_pos = width_index * rows_own + row_ids
    key_pos = jnp.concatenate([(width_index ^ s) * rows_own + row_ids for s in range(width_count)])
    seq_ends = jnp.cumsum(seq_lengths[0])
    seg_all = jnp.sum((key_pos[:, None] >= seq_ends[None, :]).astype(jnp.int32), axis=1)
    seg_query = seg_all[:rows_own]
    distance = jnp.maximum(query_pos[:, None] - key_pos[None, :], 0)
    allowed = (seg_query[:, None] == seg_all[None, :]) & (key_pos[None, :] <= query_pos[:, None])
    decay_term = jnp.where(allowed, jnp.log1p(distance.astype(jnp.float32)), 1e30)

    attended = attend(queries, keys_all, values_all, slopes, decay_term)
    proj_part = jnp.dot(attended, w_proj, preferred_element_type=jnp.float32)
    hidden_one = x_vals + (proj_part + hop(proj_part, "heads", 1))
    norm_second, back_second = jax.vjp(rms_norm, hidden_one, gain_two)
    xn_two = norm_second.astype(jnp.bfloat16)

    tokens = rows_everywhere(own_half_first(xn_two, head_index, 0), half)
    logits = jnp.einsum("ed,std->set", w_route_t, tokens, preferred_element_type=jnp.float32)
    expert_ids = jnp.arange(expert_total, dtype=jnp.int32)
    chosen = [
        jnp.sum(
            jnp.where(routes_all[:, k, None, :] == expert_ids[None, :, None], logits, 0.0), axis=1
        )
        for k in range(2)
    ]
    top_logit = jnp.maximum(chosen[0], chosen[1])
    gate_exp = [jnp.exp(c - top_logit) for c in chosen]
    gate_sum = gate_exp[0] + gate_exp[1]
    gates = [g / gate_sum for g in gate_exp]
    earlier = (row_ids[:, None] < row_ids[None, :]).astype(jnp.bfloat16)
    slot_ids = jnp.arange(slot_cap, dtype=jnp.int32)
    slots_picks = []
    slots_y = []
    slots_back = []
    gate_rows = []
    sums_in = []
    sums_out = []
    for e in range(local_experts):
        expert_id = dp_index * local_experts + e
        named = [routes_all[:, k] == expert_id for k in range(2)]
        member = named[0] | named[1]
        rank = jnp.dot(
            member.astype(jnp.bfloat16), earlier, preferred_element_type=jnp.float32
        ).astype(jnp.int32)
        place = jnp.where(member, rank, -1)
        picks = place[:, None, :] == slot_ids[None, :, None]
        picks_low = picks.astype(jnp.bfloat16)
        gate_token = jnp.where(named[0], gates[0], jnp.where(named[1], gates[1], 0.0))
        gate_slot = jnp.sum(jnp.where(picks, gate_token[:, None, :], 0.0), axis=2)
        rows_in = jnp.einsum(
            "sct,std->scd", picks_low, tokens, preferred_element_type=jnp.float32
        ).astype(jnp.bfloat16)
        rows_cot = jnp.einsum(
            "sct,std->scd", picks_low, cot_rows_all, preferred_element_type=jnp.float32
        )
        grad_rows = (gate_slot[:, :, None] * rows_cot).astype(jnp.bfloat16).reshape(-1, D)
        rows_in = rows_in.reshape(-1, D)
        pre_act = jnp.dot(rows_in, w_first[e], preferred_element_type=jnp.float32)
        activated, gelu_back = jax.vjp(jax.nn.gelu, pre_act)
        act_low = activated.astype(jnp.bfloat16)
        part_y = lax.dot_general(
            act_low, w_second_t[e], (((1,), (1,)), ((), ())), preferred_element_type=jnp.float32
        ).reshape(dp_count, slot_cap, D)
        gate_dot = jnp.sum(part_y * rows_cot, axis=2)
        gate_rows.append(jnp.sum(jnp.where(picks, gate_dot[:, :, None], 0.0), axis=1))
        slots_y.append((part_y * gate_slot[:, :, None]).astype(jnp.bfloat16))
        slots_picks.append(picks_low)
        grad_act = jnp.dot(grad_rows, w_second_t[e], preferred_element_type=jnp.float32)
        grad_pre = gelu_back(grad_act)[0].astype(jnp.bfloat16)
        rows_back = lax.dot_general(
            grad_pre, w_first[e], (((1,), (1,)), ((), ())), preferred_element_type=jnp.float32
        ).astype(jnp.bfloat16)
        slots_back.append(rows_back.reshape(dp_count, slot_cap, D))
        grad_second = lax.dot_general(
            grad_rows, act_low, (((0,), (0,)), ((), ())), preferred_element_type=jnp.float32
        ).astype(jnp.bfloat16)
        grad_first = lax.dot_general(
            rows_in, grad_pre, (((0,), (0,)), ((), ())), preferred_element_type=jnp.float32
        ).astype(jnp.bfloat16)
        cut = [slice(s * block_d, (s + 1) * block_d) for s in range(width_count)]
        sums_in.append(summed_pieces([grad_first[c] for c in cut], "width"))
        sums_out.append(summed_pieces([grad_second[c] for c in cut], "width"))
    expert_in_grad = jnp.stack(sums_in)
    expert_out_grad = jnp.swapaxes(jnp.stack(sums_out), 1, 2)

    all_picks = jnp.concatenate(slots_picks, axis=1)
    grad_xn_own = rows_returned(all_picks, jnp.concatenate(slots_back, axis=1), half)
    mixed_own = rows_returned(all_picks, jnp.concatenate(slots_y, axis=1), half)
    hidden_own = lax.dynamic_slice_in_dim(hidden_one, head_index * half, half, 0)
    mixed_low = (hidden_own + mixed_own).astype(jnp.bfloat16)
    mixed_out = xor_columns(both_halves(mixed_low, head_index), width_count, width_index)

    gate_parts = jnp.stack(gate_rows, axis=1)
    gate_pieces = [gate_parts[0]] + [hop(gate_parts[s], "dp", s) for s in range(1, dp_count)]
    gate_grad = []
    for k in range(2):
        found = 0.0
        for s in range(dp_count):
            for e in range(local_experts):
                match = routes_own[k] == (dp_index ^ s) * local_experts + e
                found = found + jnp.where(match, gate_pieces[s][e], 0.0)
        gate_grad.append(found)
    gate_vals = own_half_first(jnp.stack([gates[0][0], gates[1][0]]), head_index, 1)
    gate_grad = own_half_first(jnp.stack(gate_grad), head_index, 1)
    gate_grad = gate_grad + hop(gate_grad, "heads", 1)
    chosen_grad = gate_vals * (gate_grad - jnp.sum(gate_vals * gate_grad, axis=0, keepdims=True))
    logit_grad_t = jnp.sum(
        jnp.where(routes.T[:, None, :] == expert_ids[None, :, None], chosen_grad[:, None, :], 0.0),
        axis=0,
    )
    router_full_t = jnp.dot(logit_grad_t, xn_two.astype(jnp.float32), precision=highest)
    grad_xn_two = both_halves(grad_xn_own, head_index) + lax.dot_general(
        logit_grad_t,
        w_route_t.astype(jnp.float32),
        (((0,), (0,)), ((), ())),
        precision=highest,
    )
    back_hidden, gain_two_grad = back_second(grad_xn_two)
    grad_hidden = grad_out + back_hidden
    grad_branch = grad_hidden.astype(jnp.bfloat16)
    proj_grad = lax.dot_general(
        attended, grad_branch, (((0,), (0,)), ((), ())), preferred_element_type=jnp.float32
    ).astype(jnp.bfloat16)
    grad_att = lax.dot_general(
        grad_branch, w_proj, (((1,), (1,)), ((), ())), preferred_element_type=jnp.float32
    ).astype(jnp.bfloat16)
    query_grad, key_grad, value_grad, slope_grad = attend_back(
        queries, keys_all, values_all, slopes, decay_term, grad_att
    )
    kv_both = jnp.stack([key_grad, value_grad]).astype(jnp.bfloat16)
    kv_grad = summed_pieces(
        [kv_both[:, s * rows_own : (s + 1) * rows_own] for s in range(width_count)], "width"
    ).astype(jnp.bfloat16)
    qkv_cot = jnp.concatenate([query_grad[None], kv_grad], axis=0)
    grad_xn_part = jnp.einsum("jrc,jdc->rd", qkv_cot, w_qkv, preferred_element_type=jnp.float32)
    grad_xn_one = grad_xn_part + hop(grad_xn_part, "heads", 1)
    qkv_full_grad = jnp.einsum(
        "rd,jrc->jdc", xn_one, qkv_cot, preferred_element_type=jnp.float32
    ).astype(jnp.bfloat16)
    back_input, gain_one_grad = back_first(grad_xn_one)
    input_grad = xor_columns(grad_hidden + back_input, width_count, width_index)

    grad_chunks = [
        jnp.concatenate(
            [
                qkv_full_grad[:, c].reshape(3 * block_d, heads_cols),
                beside(proj_grad[:, c]),
            ],
            axis=0,
        )
        for c in cut
    ]
    own_grads = summed_pieces(grad_chunks, "width").astype(jnp.bfloat16)
    part_rows = own_grads.shape[0] // dp_count

    def part_of(s):
        return lax.dynamic_slice_in_dim(own_grads, (dp_index ^ s) * part_rows, part_rows, 0)

    grad_part = summed_pieces([part_of(s) for s in range(dp_count)], "dp").astype(jnp.bfloat16)
    grads = jnp.zeros_like(own_grads)
    for s, piece in enumerate(pieces_of(grad_part, "dp")):
        grads = lax.dynamic_update_slice_in_dim(grads, piece, (dp_index ^ s) * part_rows, 0)
    grads = grads.astype(jnp.float32)
    qkv_grad = grads[:out_from].reshape(3, block_d, heads_cols)
    out_grad = unbeside(grads[out_from:])

    tiny = jnp.concatenate([router_full_t, gain_one_grad[None], gain_two_grad[None]], axis=0)
    slope_row = jnp.pad(slope_grad, (0, block_d - slope_grad.shape[0]))[None]
    tiny_sum = summed_pieces([jnp.concatenate([tiny[:, c], slope_row], axis=0) for c in cut], "width")
    tiny_sum = summed_everywhere(tiny_sum, "dp")
    return (
        mixed_out,
        input_grad,
        tiny_sum[expert_total],
        qkv_grad,
        tiny_sum[expert_total + 2, : slope_grad.shape[0]],
        out_grad,
        tiny_sum[expert_total + 1],
        tiny_sum[:expert_total].T,
        expert_in_grad,
        expert_out_grad,
    )


def solution(mesh):
    return jax.shard_map(
        shards,
        mesh=mesh,
        in_specs=(
            P(("dp", "width"), None),
            P("dp", None),
            P(("dp", "width"), None),
            P("width"),
            P(None, "width", "heads"),
            P("heads"),
            P("heads", "width"),
            P("width"),
            P("width", None),
            P("dp", "width", "heads"),
            P("dp", "heads", "width"),
            P(("dp", "width"), None),
        ),
        out_specs=(
            P(("dp", "width"), None),
            P(("dp", "width"), None),
            P("width"),
            P(None, "width", "heads"),
            P("heads"),
            P("heads", "width"),
            P("width"),
            P("width", None),
            P("dp", "width", "heads"),
            P("dp", "heads", "width"),
        ),
        check_vma=False,
    )
```

```python
import math

import jax
import jax.numpy as jnp
from jax import lax
from jax.experimental import pallas as pl
from jax.experimental.pallas import tpu as pltpu
from jax.sharding import PartitionSpec as P

D = 768
HD = 64
CHUNK = 128


epsilon = 1e-06
highest = lax.Precision.HIGHEST


def rms_norm(values, gain_vec):
    return (
        values * lax.rsqrt(jnp.mean(values * values, axis=-1, keepdims=True) + epsilon) * gain_vec
    )


def attend_kernel(slopes_ref, q_ref, k_ref, v_ref, decay_ref, out_ref, log_sum_ref):
    pair = pl.program_id(0)
    keys = k_ref[...]
    values = v_ref[...]
    lane = lax.broadcasted_iota(jnp.int32, (CHUNK, 2 * HD), 1)

    def one_chunk(num, carry):
        rows = pl.ds(pl.multiple_of(num * CHUNK, CHUNK), CHUNK)
        query = q_ref[rows, :].astype(jnp.float32) * (1.0 / math.sqrt(HD))
        decay = decay_ref[rows, :]
        outs = []
        log_sums = []
        for head in range(2):
            own = lane // HD == head
            scores = lax.dot_general(
                jnp.where(own, query, 0.0).astype(jnp.bfloat16),
                keys,
                (((1,), (1,)), ((), ())),
                preferred_element_type=jnp.float32,
            )
            scores = scores - slopes_ref[2 * pair + head] * decay
            top = jnp.max(scores, axis=1, keepdims=True)
            exps = jnp.exp(scores - top)
            total = jnp.sum(exps, axis=1, keepdims=True)
            out = jnp.dot(exps.astype(jnp.bfloat16), values, preferred_element_type=jnp.float32)
            outs.append(out / total)
            log_sums.append(top + jnp.log(total))
        out_ref[rows, :] = jnp.where(lane < HD, outs[0], outs[1]).astype(jnp.bfloat16)
        log_sum_ref[rows, :] = jnp.where(lane < HD, log_sums[0], log_sums[1])
        return carry

    lax.fori_loop(0, q_ref.shape[0] // CHUNK, one_chunk, 0)


def attend_back_kernel(
    slopes_ref,
    q_ref,
    k_ref,
    v_ref,
    decay_ref,
    log_sum_ref,
    grad_ref,
    dq_ref,
    dk_ref,
    dv_ref,
    slope_ref,
    dk_sum,
    dv_sum,
):
    pair = pl.program_id(0)
    scale = 1.0 / math.sqrt(HD)
    keys = k_ref[...]
    values = v_ref[...]
    lane = lax.broadcasted_iota(jnp.int32, (CHUNK, 2 * HD), 1)
    dk_sum[...] = jnp.zeros_like(dk_sum)
    dv_sum[...] = jnp.zeros_like(dv_sum)
    rows_last = (((1,), (1,)), ((), ()))
    rows_first = (((0,), (0,)), ((), ()))

    def one_chunk(num, slope_sums):
        rows = pl.ds(pl.multiple_of(num * CHUNK, CHUNK), CHUNK)
        query = q_ref[rows, :].astype(jnp.float32) * scale
        grad = grad_ref[rows, :].astype(jnp.float32)
        log_sum = log_sum_ref[rows, :]
        decay = decay_ref[rows, :]
        dqs = []
        new_sums = []
        for head in range(2):
            own = lane // HD == head
            query_own = jnp.where(own, query, 0.0).astype(jnp.bfloat16)
            grad_own = jnp.where(own, grad, 0.0).astype(jnp.bfloat16)
            scores = lax.dot_general(
                query_own, keys, rows_last, preferred_element_type=jnp.float32
            )
            scores = scores - slopes_ref[2 * pair + head] * decay
            probs = jnp.exp(scores - log_sum[:, HD * head : HD * head + 1])
            grad_probs = lax.dot_general(
                grad_own, values, rows_last, preferred_element_type=jnp.float32
            )
            row_sum = jnp.sum(probs * grad_probs, axis=1, keepdims=True)
            grad_scores = (probs * (grad_probs - row_sum)).astype(jnp.bfloat16)
            dv_sum[...] += lax.dot_general(
                probs.astype(jnp.bfloat16),
                grad_own,
                rows_first,
                preferred_element_type=jnp.float32,
            )
            dk_sum[...] += lax.dot_general(
                grad_scores, query_own, rows_first, preferred_element_type=jnp.float32
            )
            dqs.append(jnp.dot(grad_scores, keys, preferred_element_type=jnp.float32))
            slope_part = jnp.sum(grad_scores.astype(jnp.float32) * decay, axis=0, keepdims=True)
            new_sums.append(slope_sums[head] + slope_part)
        dq_ref[rows, :] = (jnp.where(lane < HD, dqs[0], dqs[1]) * scale).astype(jnp.bfloat16)
        return tuple(new_sums)

    start = jnp.zeros((1, keys.shape[0]), jnp.float32)
    sums = lax.fori_loop(0, q_ref.shape[0] // CHUNK, one_chunk, (start, start))
    dk_ref[...] = dk_sum[...].astype(jnp.bfloat16)
    dv_ref[...] = dv_sum[...].astype(jnp.bfloat16)
    totals = [-jnp.sum(part, axis=1, keepdims=True) for part in sums]
    row = lax.broadcasted_iota(jnp.int32, (8, 128), 0)
    slope_ref[0] = jnp.where(row == 0, totals[0], totals[1])


def attend_specs(rows, keys):
    return {
        "slopes": pl.BlockSpec(memory_space=pltpu.SMEM),
        "rows": pl.BlockSpec((rows, 2 * HD), lambda p: (0, p)),
        "keys": pl.BlockSpec((keys, 2 * HD), lambda p: (0, p)),
        "decay": pl.BlockSpec((rows, keys), lambda p: (0, 0)),
    }


def attend_cost(rows, keys, heads, dots):
    return pl.CostEstimate(
        flops=2 * dots * heads * rows * keys * 2 * HD,
        bytes_accessed=4 * rows * keys + 8 * heads * HD * keys,
        transcendentals=heads * rows * keys,
    )


def attend(queries, keys_all, values_all, slopes, decay_term):
    rows, columns = queries.shape
    keys = keys_all.shape[0]
    spec = attend_specs(rows, keys)
    return pl.pallas_call(
        attend_kernel,
        grid=(columns // (2 * HD),),
        in_specs=[spec["slopes"], spec["rows"], spec["keys"], spec["keys"], spec["decay"]],
        out_specs=[spec["rows"], spec["rows"]],
        out_shape=[
            jax.ShapeDtypeStruct((rows, columns), jnp.bfloat16),
            jax.ShapeDtypeStruct((rows, columns), jnp.float32),
        ],
        cost_estimate=attend_cost(rows, keys, columns // HD, 2),
        compiler_params=pltpu.CompilerParams(vmem_limit_bytes=40 << 20),
        name="attend",
    )(slopes, queries, keys_all, values_all, decay_term)


def attend_back(queries, keys_all, values_all, slopes, decay_term, log_sums, grad_att):
    rows, columns = queries.shape
    keys = keys_all.shape[0]
    pairs = columns // (2 * HD)
    spec = attend_specs(rows, keys)
    dq, dk, dv, slope_tiles = pl.pallas_call(
        attend_back_kernel,
        grid=(pairs,),
        in_specs=[
            spec["slopes"],
            spec["rows"],
            spec["keys"],
            spec["keys"],
            spec["decay"],
            spec["rows"],
            spec["rows"],
        ],
        out_specs=[
            spec["rows"],
            spec["keys"],
            spec["keys"],
            pl.BlockSpec((1, 8, 128), lambda p: (p, 0, 0)),
        ],
        out_shape=[
            jax.ShapeDtypeStruct((rows, columns), jnp.bfloat16),
            jax.ShapeDtypeStruct((keys, columns), jnp.bfloat16),
            jax.ShapeDtypeStruct((keys, columns), jnp.bfloat16),
            jax.ShapeDtypeStruct((pairs, 8, 128), jnp.float32),
        ],
        scratch_shapes=[
            pltpu.VMEM((keys, 2 * HD), jnp.float32),
            pltpu.VMEM((keys, 2 * HD), jnp.float32),
        ],
        cost_estimate=attend_cost(rows, keys, columns // HD, 5),
        compiler_params=pltpu.CompilerParams(vmem_limit_bytes=48 << 20),
        name="attend_back",
    )(slopes, queries, keys_all, values_all, decay_term, log_sums, grad_att)
    return dq, dk, dv, slope_tiles[:, :2, 0].reshape(-1)


def swap_pairs(axis, step):
    return [(i, i ^ step) for i in range(lax.axis_size(axis))]


def hop(values, axis, step):
    return lax.ppermute(values, axis, swap_pairs(axis, step))


def pieces_of(values, axis):
    return [values] + [hop(values, axis, s) for s in range(1, lax.axis_size(axis))]


def summed_pieces(chunks, axis):
    total = chunks[0].astype(jnp.float32)
    for s in range(1, lax.axis_size(axis)):
        total = total + hop(chunks[s], axis, s).astype(jnp.float32)
    return total


def square_pieces(values, axis):
    if lax.axis_size(axis) != 4:
        return pieces_of(values, axis)
    cut = values.shape[0] // 2
    first, second = values[:cut], values[cut:]
    first_by = [first, hop(first, axis, 1), None, None]
    second_by = [second, None, hop(second, axis, 2), None]
    for s in (0, 1):
        first_by[s + 2] = hop(first_by[s], axis, 2)
    for s in (0, 2):
        second_by[s + 1] = hop(second_by[s], axis, 1)
    return [jnp.concatenate(both, axis=0) for both in zip(first_by, second_by)]


def square_hops(chunks, axis):
    cut = chunks[0].shape[0] // 2
    first = [chunk[:cut] for chunk in chunks]
    second = [chunk[cut:] for chunk in chunks]
    near = (first[1] + hop(first[3], axis, 2)).astype(jnp.bfloat16)
    side = (second[2] + hop(second[3], axis, 1)).astype(jnp.bfloat16)
    return [
        first[0],
        hop(first[2], axis, 2),
        hop(near, axis, 1),
        second[0],
        hop(second[1], axis, 1),
        hop(side, axis, 2),
    ]


def summed_square(found):
    halves = []
    for parts in (found[:3], found[3:]):
        parts = [part.astype(jnp.float32) for part in parts]
        halves.append(parts[0] + parts[1] + parts[2])
    return jnp.concatenate(halves, axis=0)


def summed_everywhere(values, axis):
    step = 1
    while step < lax.axis_size(axis):
        values = values + hop(values, axis, step)
        step *= 2
    return values


def xor_columns(values, count, index):
    width = values.shape[-1] // count
    bit = 1
    while bit < count:
        blocks = [values[..., (i ^ bit) * width : ((i ^ bit) + 1) * width] for i in range(count)]
        values = jnp.where((index & bit) > 0, jnp.concatenate(blocks, axis=-1), values)
        bit *= 2
    return values


def own_half_first(values, head_index, axis):
    half = values.shape[axis] // 2
    low_half = lax.slice_in_dim(values, 0, half, axis=axis)
    high_half = lax.slice_in_dim(values, half, 2 * half, axis=axis)
    return jnp.where(head_index == 0, values, jnp.concatenate([high_half, low_half], axis=axis))


def rows_everywhere(values, half):
    found = [values]
    for s in range(1, lax.axis_size("dp")):
        piece = hop(values[:half], "dp", s)
        found.append(jnp.concatenate([piece, hop(piece, "heads", 1)], axis=0))
    return jnp.stack(found)


def rows_returned(picks, slot_rows, half):
    mine, theirs = [
        jnp.einsum("sct,scd->std", part, slot_rows, preferred_element_type=jnp.float32)
        for part in (picks[:, :, :half], picks[:, :, half:])
    ]
    theirs = hop(theirs.astype(jnp.bfloat16), "heads", 1)
    chunks = (mine + theirs.astype(jnp.float32)).astype(jnp.bfloat16)
    return summed_pieces([chunks[s] for s in range(chunks.shape[0])], "dp")


def both_halves(own, head_index):
    other = hop(own, "heads", 1)
    return jnp.where(
        head_index == 0,
        jnp.concatenate([own, other], axis=0),
        jnp.concatenate([other, own], axis=0),
    )


def beside(values):
    half = values.shape[0] // 2
    return jnp.concatenate([values[:half], values[half:]], axis=1)


def unbeside(values):
    half = values.shape[1] // 2
    return jnp.concatenate([values[:, :half], values[:, half:]], axis=0)


def shards(
    inputs,
    seq_lengths,
    routes,
    norm_one,
    qkv_weight,
    slopes,
    out_weight,
    norm_two,
    router,
    expert_in,
    expert_out,
    cotangent,
):
    rows_own = inputs.shape[0]
    half = rows_own // 2
    width_count = lax.axis_size("width")
    dp_count = lax.axis_size("dp")
    width_index = lax.axis_index("width")
    dp_index = lax.axis_index("dp")
    head_index = lax.axis_index("heads")
    expert_total = router.shape[1]
    local_experts = expert_in.shape[0]
    slot_cap = 4 * rows_own // expert_total
    block_d = norm_one.shape[0]
    heads_cols = qkv_weight.shape[2]

    small = jnp.concatenate([router.T, norm_one[None], norm_two[None]], axis=0)
    small = beside(small)
    small_rows = small.shape[0]
    pack = jnp.concatenate(
        [
            qkv_weight.reshape(3 * block_d, heads_cols),
            beside(out_weight),
            jnp.pad(small, ((0, -small_rows % 16), (0, 0))),
        ],
        axis=0,
    )
    packs = square_pieces(pack, "width")
    out_from = 3 * block_d
    small_from = out_from + out_weight.shape[0] // 2
    w_qkv = jnp.concatenate(
        [piece[:out_from].reshape(3, block_d, heads_cols) for piece in packs], axis=1
    )
    w_proj = jnp.concatenate([unbeside(piece[out_from:small_from]) for piece in packs], axis=1)
    smalls = jnp.concatenate(
        [unbeside(piece[small_from : small_from + small_rows]) for piece in packs], axis=1
    )
    w_route_t = smalls[:expert_total]
    gain_one = smalls[expert_total].astype(jnp.float32)
    gain_two = smalls[expert_total + 1].astype(jnp.float32)

    x_vals = xor_columns(inputs, width_count, width_index).astype(jnp.float32)
    cot = xor_columns(cotangent, width_count, width_index)
    grad_out = cot.astype(jnp.float32)
    norm_first, back_first = jax.vjp(rms_norm, x_vals, gain_one)
    xn_one = norm_first.astype(jnp.bfloat16)
    qkv_vals = jnp.einsum("rd,jdc->jrc", xn_one, w_qkv, preferred_element_type=jnp.float32).astype(
        jnp.bfloat16
    )
    queries = qkv_vals[0]
    kv_pieces = square_pieces(qkv_vals[1:], "width")
    expert_stack = jnp.concatenate(
        [expert_in, jnp.swapaxes(expert_out, 1, 2).astype(jnp.bfloat16)], axis=0
    )
    kv_pieces, expert_stack = lax.optimization_barrier((kv_pieces, expert_stack))
    key_value = jnp.concatenate(kv_pieces, axis=1)
    keys_all = key_value[0]
    values_all = key_value[1]
    stacks = square_pieces(expert_stack, "width")
    w_first = [
        jnp.concatenate([piece[e] for piece in stacks], axis=0) for e in range(local_experts)
    ]
    w_second_t = [
        jnp.concatenate([piece[local_experts + e] for piece in stacks], axis=0)
        for e in range(local_experts)
    ]

    cot_rows_all = rows_everywhere(own_half_first(cot, head_index, 0), half)
    routes_own = own_half_first(routes.T, head_index, 1)
    routes_all = jnp.stack(pieces_of(routes_own, "dp"))

    row_ids = jnp.arange(rows_own, dtype=jnp.int32)
    query_pos = width_index * rows_own + row_ids
    key_pos = jnp.concatenate([(width_index ^ s) * rows_own + row_ids for s in range(width_count)])
    seq_ends = jnp.cumsum(seq_lengths[0])
    seg_all = jnp.sum((key_pos[:, None] >= seq_ends[None, :]).astype(jnp.int32), axis=1)
    seg_query = seg_all[:rows_own]
    distance = jnp.maximum(query_pos[:, None] - key_pos[None, :], 0)
    allowed = (seg_query[:, None] == seg_all[None, :]) & (key_pos[None, :] <= query_pos[:, None])
    decay_term = jnp.where(allowed, jnp.log1p(distance.astype(jnp.float32)), 1e30)

    attended, log_sums = attend(queries, keys_all, values_all, slopes, decay_term)
    proj_part = jnp.dot(attended, w_proj, preferred_element_type=jnp.float32)
    hidden_one = x_vals + (proj_part + hop(proj_part, "heads", 1))
    norm_second, back_second = jax.vjp(rms_norm, hidden_one, gain_two)
    xn_two = norm_second.astype(jnp.bfloat16)

    tokens = rows_everywhere(own_half_first(xn_two, head_index, 0), half)
    logits = jnp.einsum("ed,std->set", w_route_t, tokens, preferred_element_type=jnp.float32)
    expert_ids = jnp.arange(expert_total, dtype=jnp.int32)
    chosen = [
        jnp.sum(
            jnp.where(routes_all[:, k, None, :] == expert_ids[None, :, None], logits, 0.0), axis=1
        )
        for k in range(2)
    ]
    top_logit = jnp.maximum(chosen[0], chosen[1])
    gate_exp = [jnp.exp(c - top_logit) for c in chosen]
    gate_sum = gate_exp[0] + gate_exp[1]
    gates = [g / gate_sum for g in gate_exp]
    earlier = (row_ids[:, None] < row_ids[None, :]).astype(jnp.bfloat16)
    slot_ids = jnp.arange(slot_cap, dtype=jnp.int32)
    slots_picks = []
    slots_y = []
    slots_back = []
    gate_rows = []
    sums_found = []
    for e in range(local_experts):
        expert_id = dp_index * local_experts + e
        named = [routes_all[:, k] == expert_id for k in range(2)]
        member = named[0] | named[1]
        rank = jnp.dot(
            member.astype(jnp.bfloat16), earlier, preferred_element_type=jnp.float32
        ).astype(jnp.int32)
        place = jnp.where(member, rank, -1)
        picks = place[:, None, :] == slot_ids[None, :, None]
        picks_low = picks.astype(jnp.bfloat16)
        gate_token = jnp.where(named[0], gates[0], jnp.where(named[1], gates[1], 0.0))
        gate_slot = jnp.sum(jnp.where(picks, gate_token[:, None, :], 0.0), axis=2)
        rows_in = jnp.einsum(
            "sct,std->scd", picks_low, tokens, preferred_element_type=jnp.float32
        ).astype(jnp.bfloat16)
        rows_cot = jnp.einsum(
            "sct,std->scd", picks_low, cot_rows_all, preferred_element_type=jnp.float32
        )
        grad_rows = (gate_slot[:, :, None] * rows_cot).astype(jnp.bfloat16).reshape(-1, D)
        rows_in = rows_in.reshape(-1, D)
        pre_act = jnp.dot(rows_in, w_first[e], preferred_element_type=jnp.float32)
        activated, gelu_back = jax.vjp(jax.nn.gelu, pre_act)
        act_low = activated.astype(jnp.bfloat16)
        part_y = lax.dot_general(
            act_low, w_second_t[e], (((1,), (1,)), ((), ())), preferred_element_type=jnp.float32
        ).reshape(dp_count, slot_cap, D)
        gate_dot = jnp.sum(part_y * rows_cot, axis=2)
        gate_rows.append(jnp.sum(jnp.where(picks, gate_dot[:, :, None], 0.0), axis=1))
        slots_y.append((part_y * gate_slot[:, :, None]).astype(jnp.bfloat16))
        slots_picks.append(picks_low)
        grad_act = jnp.dot(grad_rows, w_second_t[e], preferred_element_type=jnp.float32)
        grad_pre = gelu_back(grad_act)[0].astype(jnp.bfloat16)
        rows_back = lax.dot_general(
            grad_pre, w_first[e], (((1,), (1,)), ((), ())), preferred_element_type=jnp.float32
        ).astype(jnp.bfloat16)
        slots_back.append(rows_back.reshape(dp_count, slot_cap, D))
        grad_second = lax.dot_general(
            grad_rows, act_low, (((0,), (0,)), ((), ())), preferred_element_type=jnp.float32
        ).astype(jnp.bfloat16)
        grad_first = lax.dot_general(
            rows_in, grad_pre, (((0,), (0,)), ((), ())), preferred_element_type=jnp.float32
        ).astype(jnp.bfloat16)
        cut = [slice(s * block_d, (s + 1) * block_d) for s in range(width_count)]
        sums_found.append(
            square_hops(
                [jnp.concatenate([grad_first[c], grad_second[c]], axis=0) for c in cut], "width"
            )
        )
    all_picks = jnp.concatenate(slots_picks, axis=1)
    grad_xn_own = rows_returned(all_picks, jnp.concatenate(slots_back, axis=1), half)
    grad_xn_own, slots_y = lax.optimization_barrier((grad_xn_own, slots_y))
    mixed_own = rows_returned(all_picks, jnp.concatenate(slots_y, axis=1), half)
    hidden_own = lax.dynamic_slice_in_dim(hidden_one, head_index * half, half, 0)
    mixed_low = (hidden_own + mixed_own).astype(jnp.bfloat16)
    mixed_out = xor_columns(both_halves(mixed_low, head_index), width_count, width_index)

    gate_parts = jnp.stack(gate_rows, axis=1)
    gate_pieces = [gate_parts[0]] + [hop(gate_parts[s], "dp", s) for s in range(1, dp_count)]
    gate_grad = []
    for k in range(2):
        found = 0.0
        for s in range(dp_count):
            for e in range(local_experts):
                match = routes_own[k] == (dp_index ^ s) * local_experts + e
                found = found + jnp.where(match, gate_pieces[s][e], 0.0)
        gate_grad.append(found)
    gate_vals = own_half_first(jnp.stack([gates[0][0], gates[1][0]]), head_index, 1)
    gate_grad = own_half_first(jnp.stack(gate_grad), head_index, 1)
    gate_grad = gate_grad + hop(gate_grad, "heads", 1)
    chosen_grad = gate_vals * (gate_grad - jnp.sum(gate_vals * gate_grad, axis=0, keepdims=True))
    logit_grad_t = jnp.sum(
        jnp.where(routes.T[:, None, :] == expert_ids[None, :, None], chosen_grad[:, None, :], 0.0),
        axis=0,
    )
    router_full_t = jnp.dot(logit_grad_t, xn_two.astype(jnp.float32), precision=highest)
    grad_xn_two = both_halves(grad_xn_own, head_index) + lax.dot_general(
        logit_grad_t,
        w_route_t.astype(jnp.float32),
        (((0,), (0,)), ((), ())),
        precision=highest,
    )
    back_hidden, gain_two_grad = back_second(grad_xn_two)
    grad_hidden = grad_out + back_hidden
    grad_branch = grad_hidden.astype(jnp.bfloat16)
    proj_grad = lax.dot_general(
        attended, grad_branch, (((0,), (0,)), ((), ())), preferred_element_type=jnp.float32
    ).astype(jnp.bfloat16)
    grad_att = lax.dot_general(
        grad_branch, w_proj, (((1,), (1,)), ((), ())), preferred_element_type=jnp.float32
    ).astype(jnp.bfloat16)
    query_grad, key_grad, value_grad, slope_grad = attend_back(
        queries, keys_all, values_all, slopes, decay_term, log_sums, grad_att
    )
    sums_found, key_grad, value_grad = lax.optimization_barrier((sums_found, key_grad, value_grad))
    kv_grad = summed_square(
        square_hops(
            [
                jnp.stack([part[s * rows_own : (s + 1) * rows_own] for part in (key_grad, value_grad)])
                for s in range(width_count)
            ],
            "width",
        )
    ).astype(jnp.bfloat16)
    expert_sums = jnp.stack([summed_square(found) for found in sums_found])
    expert_in_grad = expert_sums[:, :block_d]
    expert_out_grad = jnp.swapaxes(expert_sums[:, block_d:], 1, 2)
    qkv_cot = jnp.concatenate([query_grad[None], kv_grad], axis=0)
    grad_xn_part = jnp.einsum("jrc,jdc->rd", qkv_cot, w_qkv, preferred_element_type=jnp.float32)
    grad_xn_one = grad_xn_part + hop(grad_xn_part, "heads", 1)
    qkv_full_grad = jnp.einsum(
        "rd,jrc->jdc", xn_one, qkv_cot, preferred_element_type=jnp.float32
    ).astype(jnp.bfloat16)
    back_input, gain_one_grad = back_first(grad_xn_one)
    input_grad = xor_columns(grad_hidden + back_input, width_count, width_index)

    grad_chunks = [
        jnp.concatenate(
            [
                qkv_full_grad[:, c].reshape(3 * block_d, heads_cols),
                beside(proj_grad[:, c]),
            ],
            axis=0,
        )
        for c in cut
    ]
    own_grads = summed_square(square_hops(grad_chunks, "width")).astype(jnp.bfloat16)
    tiny = jnp.concatenate([router_full_t, gain_one_grad[None], gain_two_grad[None]], axis=0)
    slope_row = jnp.pad(slope_grad, (0, block_d - slope_grad.shape[0]))[None]
    tiny_sum = summed_pieces([jnp.concatenate([tiny[:, c], slope_row], axis=0) for c in cut], "width")
    tiny_sum = summed_everywhere(tiny_sum, "dp")
    part_rows = own_grads.shape[0] // dp_count

    def part_of(s):
        return lax.dynamic_slice_in_dim(own_grads, (dp_index ^ s) * part_rows, part_rows, 0)

    grad_part = summed_pieces([part_of(s) for s in range(dp_count)], "dp").astype(jnp.bfloat16)
    grads = jnp.zeros_like(own_grads)
    for s, piece in enumerate(pieces_of(grad_part, "dp")):
        grads = lax.dynamic_update_slice_in_dim(grads, piece, (dp_index ^ s) * part_rows, 0)
    grads = grads.astype(jnp.float32)
    qkv_grad = grads[:out_from].reshape(3, block_d, heads_cols)
    out_grad = unbeside(grads[out_from:])

    return (
        mixed_out,
        input_grad,
        tiny_sum[expert_total],
        qkv_grad,
        tiny_sum[expert_total + 2, : slope_grad.shape[0]],
        out_grad,
        tiny_sum[expert_total + 1],
        tiny_sum[:expert_total].T,
        expert_in_grad,
        expert_out_grad,
    )


def solution(mesh):
    return jax.shard_map(
        shards,
        mesh=mesh,
        in_specs=(
            P(("dp", "width"), None),
            P("dp", None),
            P(("dp", "width"), None),
            P("width"),
            P(None, "width", "heads"),
            P("heads"),
            P("heads", "width"),
            P("width"),
            P("width", None),
            P("dp", "width", "heads"),
            P("dp", "heads", "width"),
            P(("dp", "width"), None),
        ),
        out_specs=(
            P(("dp", "width"), None),
            P(("dp", "width"), None),
            P("width"),
            P(None, "width", "heads"),
            P("heads"),
            P("heads", "width"),
            P("width"),
            P("width", None),
            P("dp", "width", "heads"),
            P("dp", "heads", "width"),
        ),
        check_vma=False,
    )
```
